32 devices in a mesh: qrow: 4 (over x, core), qcol: 4 (over z), grp: 2 (over y).
Axes of the slice: x: 2, y: 2, z: 4, core: 2. Of those that a mesh axis runs over, the one named last changes fastest.
Arguments:
- density: float32 [512, 3, 128, 128], P(('qrow', 'qcol', 'grp')), may hold values from -1 to 1.5, as said below
- pattern: int32 [512, 3], P(('qrow', 'qcol', 'grp')), may hold values from 0 to 1, as said below
- qm_sites: float32 [4, 512], P(None, ('qrow', 'qcol', 'grp')), may hold values from 0 to 8, as said below
- positions: float32 [3, 8, 8, 4, 128], P(None, 'qrow', 'qcol', 'grp'), may hold values from 0 to 1
- atom_types: int32 [8, 8, 4, 128], P('qrow', 'qcol', 'grp'), may hold values from 0 to 7
- charges: float32 [8, 8, 4, 128], P('qrow', 'qcol', 'grp'), may hold values from -4 to 4
- eps_table: float32 [8], replicated, may hold values from 0.2 to 2
- embed_atoms: int32 [32, 32, 128], P(('qrow', 'qcol', 'grp')), may hold values from 0 to 1023
- embed_counts: int32 [32, 32], P(('qrow', 'qcol', 'grp')), may hold values from 0 to 128, as said below
Outputs:
- purified: float32 [512, 3, 128, 128], P(('qrow', 'qcol', 'grp'))
- mm_force: float32 [3, 8, 8, 4, 128], P(None, 'qrow', 'qcol', 'grp')
The draws below stay inside these ranges and needn't reach their ends.
Inputs may be any that keep to these rules, and one draw needn't show every extreme that they name: `pattern`: column 1 is 1 in every block row; column 0 is 1 in every block row i with i mod 16 < 1, and column 2 in every block row i with i mod 16 >= 15. `density`: dominant diagonal near 0.5 with small entries elsewhere. `qm_sites`: centres lie in the MM box; the fourth row lies in 0.2 to 0.8. `embed_counts`: one owner, drawn from the seed, receives 128 atoms from every device.
All inputs are finite; a program needn't handle non-finite values.
Results may differ from the reference program's by a relative error of at most 0.0003.
Values sent between devices are 32-bit elements; how exact they have to be, the bound alone decides.
A program may use at most 128 MiB of HBM per device.

```python
import math
import jax
import jax.numpy as jnp
from jax import lax

BS = 128
W = 1
NBAND = 3
RB = 16
NBLK = 512
ITERS = 6
CX = 2
CY = 2
CZ = 2
M = 128
NTYPE = 8
CAP = 128
ATOMS_DEV = 1024
NX = 8
NY = 8
NZ = 4
N_QROW = 4
N_QCOL = 4
N_GRP = 2
DEVICES = 32


def draw_density(key, part):
    full_shape = (NBLK, NBAND, BS, BS)
    noise_key, diag_key = jax.random.split(key)
    spread = 0.12 / math.sqrt(NBAND * BS)
    noise_part = spread * jax.random.normal(noise_key, full_shape, jnp.float32)
    levels = jax.random.uniform(diag_key, (NBLK, BS), jnp.float32, 0.45, 0.55)
    band_pick = (jnp.arange(NBAND) == W).astype(jnp.float32)
    identity = jnp.eye(BS, dtype=jnp.float32)
    return noise_part + band_pick[None, :, None, None] * identity[None, None] * levels[:, None, :, None]


def draw_pattern(key, part):
    coin_flips = jax.random.randint(key, (NBLK, NBAND), 0, 2, dtype=jnp.int32)
    columns = jnp.arange(NBAND, dtype=jnp.int32)[None, :]
    rows_in = (jnp.arange(NBLK, dtype=jnp.int32) % RB)[:, None]
    forced = (columns == W) | (columns == 0) & (rows_in < W) | (columns == NBAND - 1) & (rows_in >= RB - W)
    return jnp.where(forced, 1, coin_flips).astype(jnp.int32)


def draw_qm_sites(key, part):
    unit_draw = jax.random.uniform(key, (4, NBLK), jnp.float32)
    low_ends = jnp.array([0.0, 0.0, 0.0, 0.2], dtype=jnp.float32)
    span_list = jnp.array([NX, NY, NZ, 0.6], dtype=jnp.float32)
    return low_ends[:, None] + span_list[:, None] * unit_draw


def draw_embed_counts(key, part):
    hot_key, fill_key = jax.random.split(key)
    hottest = jax.random.randint(hot_key, (), 0, DEVICES, dtype=jnp.int32)
    load_draw = jax.random.randint(fill_key, (DEVICES, DEVICES), 0, CAP // 2 + 1, dtype=jnp.int32)
    columns = jnp.arange(DEVICES, dtype=jnp.int32)[None, :]
    return jnp.where(columns == hottest, CAP, load_draw).astype(jnp.int32)


def set_ends(result, stream_key, low, top_value):
    longest = result.shape.index(max(result.shape))
    spots = []
    for shift in (0, 1):
        where = [jax.random.randint(jax.random.fold_in(stream_key, axis), (), 0, length) for axis, length in enumerate(result.shape)]
        where[longest] = (where[longest] + shift) % result.shape[longest]
        spots.append(tuple(where))
    return result.at[spots[0]].set(low).at[spots[1]].set(top_value)


def block_scale(stream_key, dims, shards, low, top_value):
    factor_of, own = 1.0, jax.random.fold_in(stream_key, 6)
    for axis_at, blocks in shards:
        draws = jnp.exp(jax.random.uniform(jax.random.fold_in(own, axis_at), (blocks,), jnp.float32, low / len(shards), top_value / len(shards)))
        factor_of = factor_of * jnp.repeat(draws, dims[axis_at] // blocks).reshape([-1 if axis == axis_at else 1 for axis in range(len(dims))])
    return factor_of


def centred(stream_key, dims, width, most, shards=(), kind=jnp.bfloat16):
    values = jax.random.normal(stream_key, dims, jnp.float32) * width
    if len(shards) > 0:
        values = block_scale(stream_key, dims, shards, -0.22, 0.18) * values
    return jnp.clip(values, min=-most, max=most).astype(kind)


def setup_inputs(seed: int = 0) -> dict:
    keys = jax.random.split(jax.random.key(seed), 10)
    return {
        "density": draw_density(jax.random.fold_in(keys[9], 71), 0),
        "pattern": draw_pattern(jax.random.fold_in(keys[9], 71), 0),
        "qm_sites": draw_qm_sites(jax.random.fold_in(keys[9], 71), 0),
        "positions": jnp.clip(1.0 * jax.random.uniform(keys[3], (3, NX, NY, NZ, M), jnp.float32) ** block_scale(keys[3], (3, NX, NY, NZ, M), ((1, 4), (2, 4), (3, 2)), -0.2, 0.2), 0.0, 1.0),
        "atom_types": set_ends(jax.random.randint(keys[4], (NX, NY, NZ, M), 0, NTYPE), jax.random.fold_in(keys[4], 1), 0, NTYPE - 1).astype(jnp.int32),
        "charges": centred(keys[5], (NX, NY, NZ, M), 0.8, 4.0, ((0, 4), (1, 4), (2, 2)), jnp.float32),
        "eps_table": jnp.clip(jnp.exp(jax.random.uniform(keys[6], (NTYPE,), jnp.float32, math.log(0.2), math.log(2.0))), 0.2, 2.0),
        "embed_atoms": set_ends(jax.random.randint(keys[7], (DEVICES, DEVICES, CAP), 0, ATOMS_DEV), jax.random.fold_in(keys[7], 1), 0, ATOMS_DEV - 1).astype(jnp.int32),
        "embed_counts": draw_embed_counts(jax.random.fold_in(keys[9], 71), 0),
    }


SIGMA_SQ = 0.25
EMBED = 20.0
SOFTEN = 1.0

def keep_of(pattern, first_row, total_rows):
    row_ids = first_row + jnp.arange(pattern.shape[0], dtype=jnp.int32)[:, None]
    column_ids = row_ids + jnp.arange(pattern.shape[1], dtype=jnp.int32)[None, :] - W
    inside = (column_ids >= 0) & (column_ids < total_rows) & (pattern > 0)
    return jnp.where(inside, 1.0, 0.0).astype(jnp.float32)

def band_window(extended, row_count, half_band):
    width_band = 2 * half_band + 1
    window_rows = []
    for window_row in range(width_band):
        entries = []
        for target in range(width_band):
            offset = target - window_row + half_band
            block_piece = extended[window_row:window_row + row_count, min(max(offset, 0), width_band - 1)]
            if 0 <= offset < width_band:
                entries.append(block_piece)
            else:
                entries.append(jnp.zeros_like(block_piece))
        window_rows.append(jnp.stack(entries, axis=1))
    return jnp.stack(window_rows, axis=1)

def band_product(left_band, extended, keep_mask):
    row_count = left_band.shape[0]
    half_band = (left_band.shape[1] - 1) // 2
    window = band_window(extended, row_count, half_band)
    product = jnp.einsum('rapk,radkq->rdpq', left_band, window, precision=lax.Precision.HIGHEST)
    return product * keep_mask[:, :, None, None]

def reference_product(left_band, right_band, keep_mask):
    padded = jnp.pad(right_band, ((W, W), (0, 0), (0, 0), (0, 0)))

    def one_row(row_index):
        extended = lax.dynamic_slice_in_dim(padded, row_index, 2 * W + 1, 0)
        left_row = lax.dynamic_slice_in_dim(left_band, row_index, 1, 0)
        keep_row = lax.dynamic_slice_in_dim(keep_mask, row_index, 1, 0)
        return band_product(left_row, extended, keep_row)[0]
    return lax.map(one_row, jnp.arange(NBLK, dtype=jnp.int32))

def pair_force(own_cells, neighbour, offsets):
    delta_list = [own_cells[axis_id][..., :, None] - neighbour[axis_id][..., None, :] - offsets[axis_id] for axis_id in range(3)]
    distance_sq = delta_list[0] * delta_list[0] + delta_list[1] * delta_list[1] + delta_list[2] * delta_list[2]
    weight_pair = own_cells[3][..., :, None] * neighbour[3][..., None, :] * jnp.exp(-distance_sq / SIGMA_SQ)
    return jnp.stack([lax.optimization_barrier(jnp.sum(weight_pair * component, axis=-1)) for component in delta_list], axis=0)

def embed_term(coords, charge_row, centers, block_charge):
    gap_list = [coords[axis_id][:, None, :] - centers[axis_id][:, :, None] for axis_id in range(3)]
    total_sq = gap_list[0] * gap_list[0] + gap_list[1] * gap_list[1] + gap_list[2] * gap_list[2] + SOFTEN
    factor = block_charge[:, :, None] / (total_sq * jnp.sqrt(total_sq))
    return jnp.stack([EMBED * charge_row * lax.optimization_barrier(jnp.sum(factor * gap_part, axis=1)) for gap_part in gap_list], axis=0)

def by_device(field):
    components = field.shape[0]
    split_view = field.reshape(components, N_QROW, CX, N_QCOL, CY, N_GRP, CZ, M)
    return split_view.transpose(1, 3, 5, 0, 2, 4, 6, 7).reshape(N_QROW * N_QCOL * N_GRP, components, CX * CY * CZ * M)

def from_device(field):
    components = field.shape[1]
    split_view = field.reshape(N_QROW, N_QCOL, N_GRP, components, CX, CY, CZ, M)
    return split_view.transpose(3, 0, 4, 1, 5, 2, 6, 7).reshape(components, NX, NY, NZ, M)

def reference(density, pattern, qm_sites, positions, atom_types, charges, eps_table, embed_atoms, embed_counts):
    keep_mask = keep_of(pattern, 0, NBLK)
    current = density * keep_mask[:, :, None, None]
    for sweep_index in range(ITERS):
        square = reference_product(current, current, keep_mask)
        cube_term = reference_product(square, current, keep_mask)
        current = 3.0 * square - 2.0 * cube_term
    purified = current
    diag_mean = lax.optimization_barrier(jnp.mean(jnp.diagonal(current[:, W], axis1=1, axis2=2), axis=1))
    qm_charge = qm_sites[3] - diag_mean
    type_ids = jnp.arange(NTYPE, dtype=jnp.int32)[:, None, None, None, None]
    strength = jnp.sqrt(lax.optimization_barrier(jnp.sum(jnp.where(atom_types[None] == type_ids, eps_table[:, None, None, None, None], 0.0), axis=0)))
    stacked = jnp.concatenate([positions, strength[None]], axis=0)
    force_total = jnp.zeros_like(positions)
    for shift_x in (-1, 0, 1):
        for shift_y in (-1, 0, 1):
            for shift_z in (-1, 0, 1):
                neighbour = jnp.roll(stacked, (-shift_x, -shift_y, -shift_z), axis=(1, 2, 3))
                force_total = force_total + pair_force(stacked, neighbour, (shift_x, shift_y, shift_z))
    grid_shape = positions.shape[1:]
    coords = jnp.stack([positions[axis_id] + lax.broadcasted_iota(jnp.int32, grid_shape, axis_id).astype(jnp.float32) for axis_id in range(3)], axis=0)
    payload = by_device(jnp.concatenate([coords, charges[None]], axis=0))
    device_count = N_QROW * N_QCOL * N_GRP
    centers = qm_sites[:3].reshape(3, device_count, RB)
    owner_charge = qm_charge.reshape(device_count, RB)

    def per_source(inputs):
        rows_payload, atom_list, count_list = inputs
        chosen = jnp.take(rows_payload, atom_list, axis=1)
        live = jnp.arange(CAP, dtype=jnp.int32)[None, :] < count_list[:, None]
        charge_row = jnp.where(live, chosen[3], 0.0)
        force_rows = embed_term(chosen[:3], charge_row, centers, owner_charge)
        empty = jnp.zeros((3, rows_payload.shape[1]), jnp.float32)
        return empty.at[:, atom_list.reshape(-1)].add(force_rows.reshape(3, -1))
    embed_force = from_device(lax.map(per_source, (payload, embed_atoms, embed_counts)))
    return (purified, force_total + embed_force)
```

```python
import functools
import math

import jax
import jax.numpy as jnp
from jax import lax
from jax.experimental import pallas as pl
from jax.experimental.pallas import tpu as pltpu
from jax.sharding import PartitionSpec as P

W = 1
ITERS = 6


SIGMA_SQ = 0.25
EMBED = 20.0
SOFTEN = 1.0
MESH = pl.DeviceIdType.MESH
SCALE = math.sqrt(1.0 / (SIGMA_SQ * math.log(2.0)))


def padded(cells, sides, width):
    for axis, dim in sides:
        count = lax.axis_size(axis)
        head = lax.slice_in_dim(cells, 0, width, axis=dim)
        tail = lax.slice_in_dim(cells, cells.shape[dim] - width, cells.shape[dim], axis=dim)
        cells = jnp.concatenate(
            [
                lax.ppermute(tail, axis, [(i, (i + 1) % count) for i in range(count)]),
                cells,
                lax.ppermute(head, axis, [((i + 1) % count, i) for i in range(count)]),
            ],
            axis=dim,
        )
    return cells


def keep_of(pattern, first_row, total_rows):
    row_ids = first_row + jnp.arange(pattern.shape[0], dtype=jnp.int32)[:, None]
    column_ids = row_ids + jnp.arange(pattern.shape[1], dtype=jnp.int32)[None, :] - W
    inside = (column_ids >= 0) & (column_ids < total_rows) & (pattern > 0)
    return jnp.where(inside, 1.0, 0.0).astype(jnp.float32)


def split(value):
    high = value.astype(jnp.bfloat16)
    return high, (value - high.astype(jnp.float32)).astype(jnp.bfloat16)


def purify_kernel(
    sizes, keep_ref, density_ref, out_ref, diag_ref, high, low, outbox, inbox, send_sem, recv_sem
):
    rows, bs = density_ref.shape[0], density_ref.shape[2]
    n_col, n_grp = sizes[1], sizes[2]
    total = sizes[0] * n_col * n_grp
    me = (lax.axis_index("qrow") * n_col + lax.axis_index("qcol")) * n_grp + lax.axis_index("grp")
    has_prev, has_next = me > 0, me < total - 1

    def place(index):
        return (index // (n_col * n_grp), (index // n_grp) % n_col, index % n_grp)

    to_prev, to_next = place(jnp.maximum(me - 1, 0)), place(jnp.minimum(me + 1, total - 1))

    def copy_prev(s):
        return pltpu.make_async_remote_copy(
            outbox.at[s, 0], inbox.at[s, 1], send_sem.at[s, 0], recv_sem.at[s, 1],
            device_id=to_prev, device_id_type=MESH)

    def copy_next(s):
        return pltpu.make_async_remote_copy(
            outbox.at[s, 1], inbox.at[s, 0], send_sem.at[s, 1], recv_sem.at[s, 0],
            device_id=to_next, device_id_type=MESH)

    barrier = pltpu.get_barrier_semaphore()

    @pl.when(has_prev)
    def _():
        pl.semaphore_signal(barrier, inc=1, device_id=to_prev, device_id_type=MESH)

    @pl.when(has_next)
    def _():
        pl.semaphore_signal(barrier, inc=1, device_id=to_next, device_id_type=MESH)

    def masked(i):
        return jnp.concatenate([density_ref[i, e] * keep_ref[i, e] for e in range(3)], axis=1)

    def put(slot, row, value):
        high[slot, row], low[slot, row] = split(value)

    first, last = masked(0), masked(rows - 1)
    outbox[0, 0] = first
    outbox[0, 1] = last
    put(0, 1, first)
    put(0, rows, last)

    pl.semaphore_wait(barrier, jnp.where(has_prev, 1, 0) + jnp.where(has_next, 1, 0))

    def send(s):
        @pl.when(has_prev)
        def _():
            copy_prev(s).start()

        @pl.when(has_next)
        def _():
            copy_next(s).start()

    send(0)
    edge = jnp.zeros((bs, 3 * bs), jnp.bfloat16)
    for slot in range(2):
        for row in (0, rows + 1):
            high[slot, row] = edge
            low[slot, row] = edge

    def fill(i, carry):
        put(0, i + 1, masked(i))
        return carry

    lax.fori_loop(1, rows - 1, fill, 0)

    def product(left, windows):
        left_high, left_low = left
        parts = []
        for tile in range(2):
            columns = slice(tile * bs, (tile + 2) * bs)
            wide_high, wide_low = windows[tile]
            both = jnp.concatenate([left_high[:, columns], left_low[:, columns]], axis=0)
            by_high = jnp.dot(both, wide_high, preferred_element_type=jnp.float32)
            by_low = jnp.dot(left_high[:, columns], wide_low, preferred_element_type=jnp.float32)
            parts.append(by_high[:bs] + (by_high[bs:] + by_low))
        return [parts[0][:, :bs], parts[0][:, bs:] + parts[1][:, :bs], parts[1][:, bs:]]

    def window(store, slot, i):
        before, here, after = store.at[slot, i], store.at[slot, i + 1], store.at[slot, i + 2]
        one = jnp.concatenate([before[:, bs:], here[:, : 2 * bs]], axis=0)
        none = jnp.zeros((bs, bs), jnp.bfloat16)
        top = jnp.concatenate([none, here[:, 2 * bs :]], axis=1)
        return one, jnp.concatenate([top, after[:, : 2 * bs]], axis=0)

    def one_row(slot, i):
        windows = list(zip(window(high, slot, i), window(low, slot, i)))
        keep = [keep_ref[i, e] for e in range(3)]
        square = [keep[e] * block for e, block in enumerate(product((high[slot, i + 1], low[slot, i + 1]), windows))]
        square = jnp.concatenate(square, axis=1)
        cube = product(split(square), windows)
        fresh = [3.0 * square[:, e * bs : (e + 1) * bs] - (2.0 * keep[e]) * cube[e] for e in range(3)]
        for e in range(3):
            out_ref[i, e] = fresh[e]
        fresh = jnp.concatenate(fresh, axis=1)
        put(1 - slot, i + 1, fresh)
        return fresh

    middle = rows // 2

    def sweep(s, carry):
        slot = lax.rem(s, 2)

        def inner(i, c):
            one_row(slot, i)
            return c

        lax.fori_loop(1, middle, inner, 0, unroll=UNROLL_A)

        @pl.when(has_prev)
        def _():
            copy_prev(s).wait_send()
            copy_next(s).wait_recv()
            put(slot, 0, inbox[s, 0])

        @pl.when(has_next)
        def _():
            copy_next(s).wait_send()
            copy_prev(s).wait_recv()
            put(slot, rows + 1, inbox[s, 1])

        top = one_row(slot, 0)
        bottom = one_row(slot, rows - 1)

        @pl.when(s < ITERS - 1)
        def _():
            outbox[s + 1, 0] = top
            outbox[s + 1, 1] = bottom
            send(s + 1)

        lax.fori_loop(middle, rows - 1, inner, 0, unroll=UNROLL_A)
        return carry

    lax.fori_loop(0, ITERS, sweep, 0)
    eye = lax.broadcasted_iota(jnp.int32, (bs, bs), 0) == lax.broadcasted_iota(jnp.int32, (bs, bs), 1)

    def diagonal(i, carry):
        diag_ref[i] = jnp.sum(jnp.where(eye, out_ref[i, W], 0.0), axis=0, keepdims=True)
        return carry

    lax.fori_loop(0, rows, diagonal, 0)


UNROLL_A = 1


def purify(density, keep_mask, sizes):
    rows, band, bs = density.shape[:3]
    vmem, smem = pl.BlockSpec(memory_space=pltpu.VMEM), pl.BlockSpec(memory_space=pltpu.SMEM)
    return pl.pallas_call(
        functools.partial(purify_kernel, sizes),
        out_shape=(
            jax.ShapeDtypeStruct(density.shape, jnp.float32),
            jax.ShapeDtypeStruct((rows, 1, bs), jnp.float32),
        ),
        in_specs=[smem, vmem],
        out_specs=(vmem, vmem),
        scratch_shapes=[
            pltpu.VMEM((2, rows + 2, bs, band * bs), jnp.bfloat16),
            pltpu.VMEM((2, rows + 2, bs, band * bs), jnp.bfloat16),
            pltpu.VMEM((ITERS, 2, bs, band * bs), jnp.float32),
            pltpu.VMEM((ITERS, 2, bs, band * bs), jnp.float32),
            pltpu.SemaphoreType.DMA((ITERS, 2)),
            pltpu.SemaphoreType.DMA((ITERS, 2)),
        ],
        compiler_params=pltpu.CompilerParams(
            collective_id=0, has_side_effects=True, vmem_limit_bytes=40 * 1024 * 1024
        ),
        cost_estimate=pl.CostEstimate(
            flops=2 * 3 * 8 * 2 * ITERS * rows * bs**3, bytes_accessed=8 * density.size, transcendentals=0
        ),
    )(keep_mask, density)


def pair_kernel(cells, around_ref, own_ref, strength_ref, out_ref, spread):
    cells_x, cells_y, cells_z = cells
    atoms = own_ref.shape[2]
    step_y = cells_z + 2
    step_x = step_y * (cells_y + 2)
    ones = jnp.ones((8, atoms), jnp.float32)
    group = 32

    def one_cell(cell, carry):
        cx, cy, cz = cell // (cells_y * cells_z), (cell // cells_z) % cells_y, cell % cells_z
        corner = cx * step_x + cy * step_y + cz
        for axis in range(3):
            row = own_ref[axis, pl.ds(cell, 1), :]
            spread[axis] = jnp.transpose(jnp.broadcast_to(row, (atoms, atoms)))

        def one_group(g, c):
            here = pl.ds(pl.multiple_of(g * group, group), group)
            mine = [spread[axis, here, :] for axis in range(3)]
            sums = [jnp.zeros((group, atoms), jnp.float32) for _ in range(3)]
            for dx in range(3):
                for dy in range(3):
                    for dz in range(3):
                        at = pl.ds(corner + dx * step_x + dy * step_y + dz, 1)
                        gap = [mine[axis] - around_ref[axis, at, :] for axis in range(3)]
                        power = around_ref[3, at, :] - (gap[0] * gap[0] + gap[1] * gap[1] + gap[2] * gap[2])
                        weight = jnp.exp2(power)
                        sums = [sums[axis] + weight * gap[axis] for axis in range(3)]
            for axis in range(3):
                spread[3 + axis, here, :] = sums[axis]
            return c

        lax.fori_loop(0, atoms // group, one_group, 0)
        strength = strength_ref[pl.ds(cell, 1), :] * (1.0 / SCALE)
        for axis in range(3):
            summed = lax.dot_general(
                ones, spread[3 + axis], (((1,), (1,)), ((), ())),
                precision=lax.Precision.HIGHEST, preferred_element_type=jnp.float32)
            out_ref[axis, pl.ds(cell, 1), :] = summed[:1] * strength
        return carry

    lax.fori_loop(0, cells_x * cells_y * cells_z, one_cell, 0)


def embed_kernel(per_owner, list_ref, table_ref, coords_ref, charge_ref, pair_ref, out_ref):
    cells, atoms = charge_ref.shape
    slots = list_ref.shape[1]
    cell_ids = lax.broadcasted_iota(jnp.int32, (16, slots), 0)
    atom_ids = lax.broadcasted_iota(jnp.int32, (atoms, slots), 0)

    def one_owner(owner, sums):
        row = list_ref[pl.ds(owner, 1), :]
        in_cell = jnp.where(cell_ids == (row >> int(math.log2(atoms))), 1.0, 0.0).astype(jnp.bfloat16)
        in_slot = jnp.where(atom_ids == (row & (atoms - 1)), 1.0, 0.0).astype(jnp.bfloat16)
        times = lax.dot_general(in_cell, in_slot, (((1,), (1,)), ((), ())), preferred_element_type=jnp.float32)
        sums = list(sums)
        for part in range(per_owner // 8):
            start = pl.ds(pl.multiple_of(owner * per_owner + part * 8, 8), 8)
            table = table_ref[start, :]
            site = [jnp.broadcast_to(table[:, k : k + 1], (8, atoms)) for k in range(4)]
            for cell in range(cells):
                gap = [coords_ref[axis, cell : cell + 1, :] - site[axis] for axis in range(3)]
                square = gap[0] * gap[0] + gap[1] * gap[1] + gap[2] * gap[2] + SOFTEN
                root = lax.rsqrt(square)
                factor = (site[3] * times[cell : cell + 1, :]) * (root * root * root)
                for axis in range(3):
                    sums[axis * cells + cell] = sums[axis * cells + cell] + factor * gap[axis]
        return tuple(sums)

    zero = jnp.zeros((8, atoms), jnp.float32)
    sums = lax.fori_loop(0, list_ref.shape[0], one_owner, (zero,) * (3 * cells))
    for axis in range(3):
        for cell in range(cells):
            force = jnp.sum(sums[axis * cells + cell], axis=0, keepdims=True)
            out_ref[axis, cell : cell + 1, :] = (
                pair_ref[axis, cell : cell + 1, :] + EMBED * charge_ref[cell : cell + 1, :] * force
            )


def per_device(
    density, pattern, qm_sites, positions, atom_types, charges, eps_table, embed_atoms, embed_counts
):
    row_count = density.shape[0]
    axes = ("qrow", "qcol", "grp")
    sizes = tuple(lax.axis_size(axis) for axis in axes)
    device_count = sizes[0] * sizes[1] * sizes[2]
    first_row = lax.axis_index(axes) * row_count
    keep_mask = keep_of(pattern, first_row, row_count * device_count)
    grid_shape = positions.shape[1:]
    cells, atoms = grid_shape[:3], grid_shape[3]
    cell_count = cells[0] * cells[1] * cells[2]
    flat = (cell_count, atoms)

    type_ids = jnp.arange(eps_table.shape[0], dtype=jnp.int32)[:, None, None, None, None]
    strength = jnp.sqrt(
        jnp.sum(
            jnp.where(atom_types[None] == type_ids, eps_table[:, None, None, None, None], 0.0),
            axis=0,
        )
    )
    stacked = jnp.concatenate([positions, jnp.log2(strength)[None]], axis=0)
    extended = padded(stacked, (("qrow", 1), ("qcol", 2), ("grp", 3)), 1)
    wide = extended.shape[1:]
    around = jnp.concatenate(
        [
            jnp.stack(
                [
                    (extended[axis] + (lax.broadcasted_iota(jnp.int32, wide, axis) - 1).astype(jnp.float32)) * SCALE
                    for axis in range(3)
                ]
            ),
            extended[3:],
        ],
        axis=0,
    ).reshape(4, -1, atoms)
    local = [lax.broadcasted_iota(jnp.int32, grid_shape, axis) for axis in range(3)]
    own = jnp.stack([(positions[axis] + local[axis].astype(jnp.float32)) * SCALE for axis in range(3)])
    coords = jnp.stack(
        [
            positions[axis] + (local[axis] + lax.axis_index(axes[axis]) * cells[axis]).astype(jnp.float32)
            for axis in range(3)
        ]
    ).reshape((3,) + flat)

    current, diagonal = purify(density, keep_mask, sizes)
    qm_charge = qm_sites[3] - jnp.mean(diagonal[:, 0], axis=1)
    table = jnp.concatenate([qm_sites[:3], qm_charge[None]], axis=0).T
    table = lax.all_gather(table, axes, axis=0, tiled=True)

    pair = pl.pallas_call(
        functools.partial(pair_kernel, cells),
        out_shape=jax.ShapeDtypeStruct((3,) + flat, jnp.float32),
        scratch_shapes=[pltpu.VMEM((6, atoms, atoms), jnp.float32)],
        compiler_params=pltpu.CompilerParams(vmem_limit_bytes=16 * 1024 * 1024),
        cost_estimate=pl.CostEstimate(
            flops=27 * 15 * cell_count * atoms * atoms, bytes_accessed=4 * around.size,
            transcendentals=27 * cell_count * atoms * atoms,
        ),
    )(around, own.reshape((3,) + flat), strength.reshape(flat))

    live = jnp.arange(embed_atoms.shape[2], dtype=jnp.int32)[None, :] < embed_counts[0][:, None]
    lists = jnp.where(live, embed_atoms[0], -1)
    force = pl.pallas_call(
        functools.partial(embed_kernel, row_count),
        out_shape=jax.ShapeDtypeStruct((3,) + flat, jnp.float32),
        compiler_params=pltpu.CompilerParams(vmem_limit_bytes=16 * 1024 * 1024),
    )(lists, table, coords, charges.reshape(flat), pair)
    return (current, force.reshape(positions.shape))


def solution(mesh):
    in_specs = (
        P(("qrow", "qcol", "grp"), None, None, None),
        P(("qrow", "qcol", "grp"), None),
        P(None, ("qrow", "qcol", "grp")),
        P(None, "qrow", "qcol", "grp", None),
        P("qrow", "qcol", "grp", None),
        P("qrow", "qcol", "grp", None),
        P(),
        P(("qrow", "qcol", "grp"), None, None),
        P(("qrow", "qcol", "grp"), None),
    )
    out_specs = (P(("qrow", "qcol", "grp"), None, None, None), P(None, "qrow", "qcol", "grp", None))
    return jax.shard_map(
        per_device, mesh=mesh, in_specs=in_specs, out_specs=out_specs, check_vma=False
    )
```

```python
import functools
import math

import jax
import jax.numpy as jnp
from jax import lax
from jax.experimental import pallas as pl
from jax.experimental.pallas import tpu as pltpu
from jax.sharding import PartitionSpec as P

W = 1
ITERS = 6


SIGMA_SQ = 0.25
EMBED = 20.0
SOFTEN = 1.0
MESH = pl.DeviceIdType.MESH
K_STACK = True
AT_ONCE = 2
SCALE = math.sqrt(1.0 / (SIGMA_SQ * math.log(2.0)))


def padded(cells, sides, width):
    for axis, dim in sides:
        count = lax.axis_size(axis)
        head = lax.slice_in_dim(cells, 0, width, axis=dim)
        tail = lax.slice_in_dim(cells, cells.shape[dim] - width, cells.shape[dim], axis=dim)
        cells = jnp.concatenate(
            [
                lax.ppermute(tail, axis, [(i, (i + 1) % count) for i in range(count)]),
                cells,
                lax.ppermute(head, axis, [((i + 1) % count, i) for i in range(count)]),
            ],
            axis=dim,
        )
    return cells


def keep_of(pattern, first_row, total_rows):
    row_ids = first_row + jnp.arange(pattern.shape[0], dtype=jnp.int32)[:, None]
    column_ids = row_ids + jnp.arange(pattern.shape[1], dtype=jnp.int32)[None, :] - W
    inside = (column_ids >= 0) & (column_ids < total_rows) & (pattern > 0)
    return jnp.where(inside, 1.0, 0.0).astype(jnp.float32)


def split(value):
    high = value.astype(jnp.bfloat16)
    return high, (value - high.astype(jnp.float32)).astype(jnp.bfloat16)


def purify_kernel(
    sizes, keep_ref, density_ref, out_ref, diag_ref, high, low, outbox, inbox, send_sem, recv_sem
):
    rows, bs = density_ref.shape[0], density_ref.shape[2]
    n_col, n_grp = sizes[1], sizes[2]
    total = sizes[0] * n_col * n_grp
    me = (lax.axis_index("qrow") * n_col + lax.axis_index("qcol")) * n_grp + lax.axis_index("grp")
    has_prev, has_next = me > 0, me < total - 1

    def place(index):
        return (index // (n_col * n_grp), (index // n_grp) % n_col, index % n_grp)

    to_prev, to_next = place(jnp.maximum(me - 1, 0)), place(jnp.minimum(me + 1, total - 1))

    def copy_prev(s):
        return pltpu.make_async_remote_copy(
            outbox.at[s, 0], inbox.at[s, 1], send_sem.at[s, 0], recv_sem.at[s, 1],
            device_id=to_prev, device_id_type=MESH)

    def copy_next(s):
        return pltpu.make_async_remote_copy(
            outbox.at[s, 1], inbox.at[s, 0], send_sem.at[s, 1], recv_sem.at[s, 0],
            device_id=to_next, device_id_type=MESH)

    barrier = pltpu.get_barrier_semaphore()

    @pl.when(has_prev)
    def _():
        pl.semaphore_signal(barrier, inc=1, device_id=to_prev, device_id_type=MESH)

    @pl.when(has_next)
    def _():
        pl.semaphore_signal(barrier, inc=1, device_id=to_next, device_id_type=MESH)

    eye = lax.broadcasted_iota(jnp.int32, (bs, bs), 0) == lax.broadcasted_iota(jnp.int32, (bs, bs), 1)
    half = jnp.where(eye, 0.5, 0.0)

    def masked(i):
        blocks = [density_ref[i, e] * keep_ref[i, e] for e in range(3)]
        blocks[W] = blocks[W] - half
        for e in range(3):
            out_ref[i, e] = blocks[e]
        return jnp.concatenate(blocks, axis=1)

    def put(slot, row, value):
        high[slot, row], low[slot, row] = split(value)

    first, last = masked(0), masked(rows - 1)
    outbox[0, 0] = first
    outbox[0, 1] = last
    put(0, 1, first)
    put(0, rows, last)

    pl.semaphore_wait(barrier, jnp.where(has_prev, 1, 0) + jnp.where(has_next, 1, 0))

    def send(s):
        @pl.when(has_prev)
        def _():
            copy_prev(s).start()

        @pl.when(has_next)
        def _():
            copy_next(s).start()

    send(0)
    edge = jnp.zeros((bs, 3 * bs), jnp.bfloat16)
    for slot in range(2):
        for row in (0, rows + 1):
            high[slot, row] = edge
            low[slot, row] = edge

    def fill(i, carry):
        put(0, i + 1, masked(i))
        return carry

    lax.fori_loop(1, rows - 1, fill, 0)

    def product(left, windows):
        left_high, left_low = left
        parts = []
        for tile in range(2):
            columns = slice(tile * bs, (tile + 2) * bs)
            wide_high, wide_low = windows[tile]
            if K_STACK:
                deep = jnp.concatenate([left_high[:, columns], left_low[:, columns], left_high[:, columns]], axis=1)
                wide = jnp.concatenate([wide_high, wide_high, wide_low], axis=0)
                parts.append(jnp.dot(deep, wide, preferred_element_type=jnp.float32))
            else:
                both = jnp.concatenate([left_high[:, columns], left_low[:, columns]], axis=0)
                by_high = jnp.dot(both, wide_high, preferred_element_type=jnp.float32)
                by_low = jnp.dot(left_high[:, columns], wide_low, preferred_element_type=jnp.float32)
                parts.append(by_high[:bs] + (by_high[bs:] + by_low))
        return [parts[0][:, :bs], parts[0][:, bs:] + parts[1][:, :bs], parts[1][:, bs:]]

    def window(store, slot, i):
        before, here, after = store.at[slot, i], store.at[slot, i + 1], store.at[slot, i + 2]
        one = jnp.concatenate([before[:, bs:], here[:, : 2 * bs]], axis=0)
        none = jnp.zeros((bs, bs), jnp.bfloat16)
        top = jnp.concatenate([none, here[:, 2 * bs :]], axis=1)
        return one, jnp.concatenate([top, after[:, : 2 * bs]], axis=0)

    def some_rows(slot, picked):
        windows = [list(zip(window(high, slot, i), window(low, slot, i))) for i in picked]
        keeps = [[keep_ref[i, e] for e in range(3)] for i in picked]
        squares = []
        for i, pieces, keep in zip(picked, windows, keeps):
            blocks = product((high[slot, i + 1], low[slot, i + 1]), pieces)
            squares.append(split(jnp.concatenate([keep[e] * blocks[e] for e in range(3)], axis=1)))
        cubes = [product(square, pieces) for square, pieces in zip(squares, windows)]
        results = []
        for i, cube, keep in zip(picked, cubes, keeps):
            fresh = [1.5 * out_ref[i, e] - (2.0 * keep[e]) * cube[e] for e in range(3)]
            results.append((fresh, split(jnp.concatenate(fresh, axis=1))))
        for i, (fresh, (fresh_high, fresh_low)) in zip(picked, results):
            for e in range(3):
                out_ref[i, e] = fresh[e]
            high[1 - slot, i + 1] = fresh_high
            low[1 - slot, i + 1] = fresh_low
        return [jnp.concatenate(fresh, axis=1) for fresh, _ in results]

    steps = (rows - 2) // AT_ONCE

    def sweep(s, carry):
        slot = lax.rem(s, 2)

        def inner(i, c):
            some_rows(slot, [1 + AT_ONCE * i + k for k in range(AT_ONCE)])
            return c

        lax.fori_loop(0, steps // 2, inner, 0)

        @pl.when(has_prev)
        def _():
            copy_prev(s).wait_send()
            copy_next(s).wait_recv()
            put(slot, 0, inbox[s, 0])

        @pl.when(has_next)
        def _():
            copy_next(s).wait_send()
            copy_prev(s).wait_recv()
            put(slot, rows + 1, inbox[s, 1])

        top, bottom = some_rows(slot, [0, rows - 1])

        @pl.when(s < ITERS - 1)
        def _():
            outbox[s + 1, 0] = top
            outbox[s + 1, 1] = bottom
            send(s + 1)

        lax.fori_loop(steps // 2, steps, inner, 0)
        return carry

    lax.fori_loop(0, ITERS, sweep, 0)

    def diagonal(i, carry):
        block = out_ref[i, W] + half
        out_ref[i, W] = block
        diag_ref[i] = jnp.sum(jnp.where(eye, block, 0.0), axis=0, keepdims=True)
        return carry

    lax.fori_loop(0, rows, diagonal, 0)


def purify(density, keep_mask, sizes):
    rows, band, bs = density.shape[:3]
    vmem, smem = pl.BlockSpec(memory_space=pltpu.VMEM), pl.BlockSpec(memory_space=pltpu.SMEM)
    return pl.pallas_call(
        functools.partial(purify_kernel, sizes),
        out_shape=(
            jax.ShapeDtypeStruct(density.shape, jnp.float32),
            jax.ShapeDtypeStruct((rows, 1, bs), jnp.float32),
        ),
        in_specs=[smem, vmem],
        out_specs=(vmem, vmem),
        scratch_shapes=[
            pltpu.VMEM((2, rows + 2, bs, band * bs), jnp.bfloat16),
            pltpu.VMEM((2, rows + 2, bs, band * bs), jnp.bfloat16),
            pltpu.VMEM((ITERS, 2, bs, band * bs), jnp.float32),
            pltpu.VMEM((ITERS, 2, bs, band * bs), jnp.float32),
            pltpu.SemaphoreType.DMA((ITERS, 2)),
            pltpu.SemaphoreType.DMA((ITERS, 2)),
        ],
        compiler_params=pltpu.CompilerParams(
            collective_id=0, has_side_effects=True, vmem_limit_bytes=40 * 1024 * 1024
        ),
        cost_estimate=pl.CostEstimate(
            flops=2 * 3 * 8 * 2 * ITERS * rows * bs**3, bytes_accessed=8 * density.size, transcendentals=0
        ),
    )(keep_mask, density)


def pair_kernel(cells, around_ref, own_ref, strength_ref, out_ref, spread):
    cells_x, cells_y, cells_z = cells
    atoms = own_ref.shape[2]
    step_y = cells_z + 2
    step_x = step_y * (cells_y + 2)
    ones = jnp.ones((8, atoms), jnp.float32)
    group = 32

    def one_cell(cell, carry):
        cx, cy, cz = cell // (cells_y * cells_z), (cell // cells_z) % cells_y, cell % cells_z
        corner = cx * step_x + cy * step_y + cz
        for axis in range(3):
            row = own_ref[axis, pl.ds(cell, 1), :]
            spread[axis] = jnp.transpose(jnp.broadcast_to(row, (atoms, atoms)))

        def one_group(g, c):
            here = pl.ds(pl.multiple_of(g * group, group), group)
            mine = [spread[axis, here, :] for axis in range(3)]
            sums = [jnp.zeros((group, atoms), jnp.float32) for _ in range(3)]
            for dx in range(3):
                for dy in range(3):
                    for dz in range(3):
                        at = pl.ds(corner + dx * step_x + dy * step_y + dz, 1)
                        gap = [mine[axis] - around_ref[axis, at, :] for axis in range(3)]
                        power = around_ref[3, at, :] - (gap[0] * gap[0] + gap[1] * gap[1] + gap[2] * gap[2])
                        weight = jnp.exp2(power)
                        sums = [sums[axis] + weight * gap[axis] for axis in range(3)]
            for axis in range(3):
                spread[3 + axis, here, :] = sums[axis]
            return c

        lax.fori_loop(0, atoms // group, one_group, 0)
        strength = strength_ref[pl.ds(cell, 1), :] * (1.0 / SCALE)
        for axis in range(3):
            summed = lax.dot_general(
                ones, spread[3 + axis], (((1,), (1,)), ((), ())),
                precision=lax.Precision.HIGHEST, preferred_element_type=jnp.float32)
            out_ref[axis, pl.ds(cell, 1), :] = summed[:1] * strength
        return carry

    lax.fori_loop(0, cells_x * cells_y * cells_z, one_cell, 0)


def embed_kernel(per_owner, list_ref, table_ref, coords_ref, charge_ref, pair_ref, out_ref):
    cells, atoms = charge_ref.shape
    slots = list_ref.shape[1]
    cell_ids = lax.broadcasted_iota(jnp.int32, (16, slots), 0)
    atom_ids = lax.broadcasted_iota(jnp.int32, (atoms, slots), 0)

    def one_owner(owner, sums):
        row = list_ref[pl.ds(owner, 1), :]
        in_cell = jnp.where(cell_ids == (row >> int(math.log2(atoms))), 1.0, 0.0).astype(jnp.bfloat16)
        in_slot = jnp.where(atom_ids == (row & (atoms - 1)), 1.0, 0.0).astype(jnp.bfloat16)
        times = lax.dot_general(in_cell, in_slot, (((1,), (1,)), ((), ())), preferred_element_type=jnp.float32)
        sums = list(sums)
        for part in range(per_owner // 8):
            start = pl.ds(pl.multiple_of(owner * per_owner + part * 8, 8), 8)
            table = table_ref[start, :]
            site = [jnp.broadcast_to(table[:, k : k + 1], (8, atoms)) for k in range(4)]
            for cell in range(cells):
                gap = [coords_ref[axis, cell : cell + 1, :] - site[axis] for axis in range(3)]
                square = gap[0] * gap[0] + gap[1] * gap[1] + gap[2] * gap[2] + SOFTEN
                root = lax.rsqrt(square)
                factor = (site[3] * times[cell : cell + 1, :]) * (root * root * root)
                for axis in range(3):
                    sums[axis * cells + cell] = sums[axis * cells + cell] + factor * gap[axis]
        return tuple(sums)

    zero = jnp.zeros((8, atoms), jnp.float32)
    sums = lax.fori_loop(0, list_ref.shape[0], one_owner, (zero,) * (3 * cells))
    for axis in range(3):
        for cell in range(cells):
            force = jnp.sum(sums[axis * cells + cell], axis=0, keepdims=True)
            out_ref[axis, cell : cell + 1, :] = (
                pair_ref[axis, cell : cell + 1, :] + EMBED * charge_ref[cell : cell + 1, :] * force
            )


def per_device(
    density, pattern, qm_sites, positions, atom_types, charges, eps_table, embed_atoms, embed_counts
):
    row_count = density.shape[0]
    axes = ("qrow", "qcol", "grp")
    sizes = tuple(lax.axis_size(axis) for axis in axes)
    device_count = sizes[0] * sizes[1] * sizes[2]
    first_row = lax.axis_index(axes) * row_count
    keep_mask = keep_of(pattern, first_row, row_count * device_count)
    grid_shape = positions.shape[1:]
    cells, atoms = grid_shape[:3], grid_shape[3]
    cell_count = cells[0] * cells[1] * cells[2]
    flat = (cell_count, atoms)

    type_ids = jnp.arange(eps_table.shape[0], dtype=jnp.int32)[:, None, None, None, None]
    strength = jnp.sqrt(
        jnp.sum(
            jnp.where(atom_types[None] == type_ids, eps_table[:, None, None, None, None], 0.0),
            axis=0,
        )
    )
    stacked = jnp.concatenate([positions, jnp.log2(strength)[None]], axis=0)
    extended = padded(stacked, (("qrow", 1), ("qcol", 2), ("grp", 3)), 1)
    wide = extended.shape[1:]
    around = jnp.concatenate(
        [
            jnp.stack(
                [
                    (extended[axis] + (lax.broadcasted_iota(jnp.int32, wide, axis) - 1).astype(jnp.float32)) * SCALE
                    for axis in range(3)
                ]
            ),
            extended[3:],
        ],
        axis=0,
    ).reshape(4, -1, atoms)
    local = [lax.broadcasted_iota(jnp.int32, grid_shape, axis) for axis in range(3)]
    own = jnp.stack([(positions[axis] + local[axis].astype(jnp.float32)) * SCALE for axis in range(3)])
    coords = jnp.stack(
        [
            positions[axis] + (local[axis] + lax.axis_index(axes[axis]) * cells[axis]).astype(jnp.float32)
            for axis in range(3)
        ]
    ).reshape((3,) + flat)

    current, diagonal = purify(density, keep_mask, sizes)
    qm_charge = qm_sites[3] - jnp.mean(diagonal[:, 0], axis=1)
    table = jnp.concatenate([qm_sites[:3], qm_charge[None]], axis=0).T
    table = lax.all_to_all(
        jnp.broadcast_to(table.reshape(1, -1), (device_count, table.size)), axes, 0, 0, tiled=True
    ).reshape(-1, 4)

    pair = pl.pallas_call(
        functools.partial(pair_kernel, cells),
        out_shape=jax.ShapeDtypeStruct((3,) + flat, jnp.float32),
        scratch_shapes=[pltpu.VMEM((6, atoms, atoms), jnp.float32)],
        compiler_params=pltpu.CompilerParams(vmem_limit_bytes=16 * 1024 * 1024),
        cost_estimate=pl.CostEstimate(
            flops=27 * 15 * cell_count * atoms * atoms, bytes_accessed=4 * around.size,
            transcendentals=27 * cell_count * atoms * atoms,
        ),
    )(around, own.reshape((3,) + flat), strength.reshape(flat))

    live = jnp.arange(embed_atoms.shape[2], dtype=jnp.int32)[None, :] < embed_counts[0][:, None]
    lists = jnp.where(live, embed_atoms[0], -1)
    force = pl.pallas_call(
        functools.partial(embed_kernel, row_count),
        out_shape=jax.ShapeDtypeStruct((3,) + flat, jnp.float32),
        compiler_params=pltpu.CompilerParams(vmem_limit_bytes=16 * 1024 * 1024),
    )(lists, table, coords, charges.reshape(flat), pair)
    return (current, force.reshape(positions.shape))


def solution(mesh):
    in_specs = (
        P(("qrow", "qcol", "grp"), None, None, None),
        P(("qrow", "qcol", "grp"), None),
        P(None, ("qrow", "qcol", "grp")),
        P(None, "qrow", "qcol", "grp", None),
        P("qrow", "qcol", "grp", None),
        P("qrow", "qcol", "grp", None),
        P(),
        P(("qrow", "qcol", "grp"), None, None),
        P(("qrow", "qcol", "grp"), None),
    )
    out_specs = (P(("qrow", "qcol", "grp"), None, None, None), P(None, "qrow", "qcol", "grp", None))
    return jax.shard_map(
        per_device, mesh=mesh, in_specs=in_specs, out_specs=out_specs, check_vma=False
    )
```

```python
import functools
import math

import jax
import jax.numpy as jnp
from jax import lax
from jax.experimental import pallas as pl
from jax.experimental.pallas import tpu as pltpu
from jax.sharding import PartitionSpec as P

W = 1
ITERS = 6


SIGMA_SQ = 0.25
EMBED = 20.0
SOFTEN = 1.0
MESH = pl.DeviceIdType.MESH
K_STACK = True
AT_ONCE = 2
SCALE = math.sqrt(1.0 / (SIGMA_SQ * math.log(2.0)))


def padded(cells, sides, width):
    for axis, dim in sides:
        count = lax.axis_size(axis)
        head = lax.slice_in_dim(cells, 0, width, axis=dim)
        tail = lax.slice_in_dim(cells, cells.shape[dim] - width, cells.shape[dim], axis=dim)
        cells = jnp.concatenate(
            [
                lax.ppermute(tail, axis, [(i, (i + 1) % count) for i in range(count)]),
                cells,
                lax.ppermute(head, axis, [((i + 1) % count, i) for i in range(count)]),
            ],
            axis=dim,
        )
    return cells


def keep_of(pattern, first_row, total_rows):
    row_ids = first_row + jnp.arange(pattern.shape[0], dtype=jnp.int32)[:, None]
    column_ids = row_ids + jnp.arange(pattern.shape[1], dtype=jnp.int32)[None, :] - W
    inside = (column_ids >= 0) & (column_ids < total_rows) & (pattern > 0)
    return jnp.where(inside, 1.0, 0.0).astype(jnp.float32)


def split(value):
    high = value.astype(jnp.bfloat16)
    return high, (value - high.astype(jnp.float32)).astype(jnp.bfloat16)


def purify_kernel(
    sizes, keep_ref, density_ref, out_ref, diag_ref, high, low, outbox, inbox, send_sem, recv_sem
):
    rows, bs = density_ref.shape[0], density_ref.shape[2]
    n_col, n_grp = sizes[1], sizes[2]
    total = sizes[0] * n_col * n_grp
    me = (lax.axis_index("qrow") * n_col + lax.axis_index("qcol")) * n_grp + lax.axis_index("grp")
    has_prev, has_next = me > 0, me < total - 1

    def place(index):
        return (index // (n_col * n_grp), (index // n_grp) % n_col, index % n_grp)

    to_prev, to_next = place(jnp.maximum(me - 1, 0)), place(jnp.minimum(me + 1, total - 1))

    def copy_prev(s):
        return pltpu.make_async_remote_copy(
            outbox.at[s, 0], inbox.at[s, 1], send_sem.at[s, 0], recv_sem.at[s, 1],
            device_id=to_prev, device_id_type=MESH)

    def copy_next(s):
        return pltpu.make_async_remote_copy(
            outbox.at[s, 1], inbox.at[s, 0], send_sem.at[s, 1], recv_sem.at[s, 0],
            device_id=to_next, device_id_type=MESH)

    barrier = pltpu.get_barrier_semaphore()

    @pl.when(has_prev)
    def _():
        pl.semaphore_signal(barrier, inc=1, device_id=to_prev, device_id_type=MESH)

    @pl.when(has_next)
    def _():
        pl.semaphore_signal(barrier, inc=1, device_id=to_next, device_id_type=MESH)

    eye = lax.broadcasted_iota(jnp.int32, (bs, bs), 0) == lax.broadcasted_iota(jnp.int32, (bs, bs), 1)
    half = jnp.where(eye, 0.5, 0.0)

    def masked(i):
        blocks = [density_ref[i, e] * keep_ref[i, e] for e in range(3)]
        blocks[W] = blocks[W] - half
        for e in range(3):
            out_ref[i, e] = blocks[e]
        return jnp.concatenate(blocks, axis=1)

    def put(slot, row, value):
        high[slot, row], low[slot, row] = split(value)

    first, last = masked(0), masked(rows - 1)
    outbox[0, 0] = first[:, : 2 * bs]
    outbox[0, 1] = last[:, bs:]
    put(0, 1, first)
    put(0, rows, last)

    pl.semaphore_wait(barrier, jnp.where(has_prev, 1, 0) + jnp.where(has_next, 1, 0))

    def send(s):
        @pl.when(has_prev)
        def _():
            copy_prev(s).start()

        @pl.when(has_next)
        def _():
            copy_next(s).start()

    send(0)
    edge = jnp.zeros((bs, 3 * bs), jnp.bfloat16)
    for slot in range(2):
        for row in (0, rows + 1):
            high[slot, row] = edge
            low[slot, row] = edge

    def fill(i, carry):
        put(0, i + 1, masked(i))
        return carry

    lax.fori_loop(1, rows - 1, fill, 0)

    def product(left, windows):
        left_high, left_low = left
        parts = []
        for tile in range(2):
            columns = slice(tile * bs, (tile + 2) * bs)
            wide_high, wide_low = windows[tile]
            if K_STACK:
                deep = jnp.concatenate([left_high[:, columns], left_low[:, columns], left_high[:, columns]], axis=1)
                wide = jnp.concatenate([wide_high, wide_high, wide_low], axis=0)
                parts.append(jnp.dot(deep, wide, preferred_element_type=jnp.float32))
            else:
                both = jnp.concatenate([left_high[:, columns], left_low[:, columns]], axis=0)
                by_high = jnp.dot(both, wide_high, preferred_element_type=jnp.float32)
                by_low = jnp.dot(left_high[:, columns], wide_low, preferred_element_type=jnp.float32)
                parts.append(by_high[:bs] + (by_high[bs:] + by_low))
        return [parts[0][:, :bs], parts[0][:, bs:] + parts[1][:, :bs], parts[1][:, bs:]]

    def window(store, slot, i):
        before, here, after = store.at[slot, i], store.at[slot, i + 1], store.at[slot, i + 2]
        one = jnp.concatenate([before[:, bs:], here[:, : 2 * bs]], axis=0)
        none = jnp.zeros((bs, bs), jnp.bfloat16)
        top = jnp.concatenate([none, here[:, 2 * bs :]], axis=1)
        return one, jnp.concatenate([top, after[:, : 2 * bs]], axis=0)

    def some_rows(slot, picked):
        windows = [list(zip(window(high, slot, i), window(low, slot, i))) for i in picked]
        keeps = [[keep_ref[i, e] for e in range(3)] for i in picked]
        squares = []
        for i, pieces, keep in zip(picked, windows, keeps):
            blocks = product((high[slot, i + 1], low[slot, i + 1]), pieces)
            squares.append(split(jnp.concatenate([keep[e] * blocks[e] for e in range(3)], axis=1)))
        cubes = [product(square, pieces) for square, pieces in zip(squares, windows)]
        results = []
        for i, cube, keep in zip(picked, cubes, keeps):
            fresh = [1.5 * out_ref[i, e] - (2.0 * keep[e]) * cube[e] for e in range(3)]
            results.append((fresh, split(jnp.concatenate(fresh, axis=1))))
        for i, (fresh, (fresh_high, fresh_low)) in zip(picked, results):
            for e in range(3):
                out_ref[i, e] = fresh[e]
            high[1 - slot, i + 1] = fresh_high
            low[1 - slot, i + 1] = fresh_low
        return [jnp.concatenate(fresh, axis=1) for fresh, _ in results]

    steps = (rows - 2) // AT_ONCE

    def sweep(s, carry):
        slot = lax.rem(s, 2)

        def inner(i, c):
            some_rows(slot, [1 + AT_ONCE * i + k for k in range(AT_ONCE)])
            return c

        lax.fori_loop(0, steps // 2, inner, 0)

        @pl.when(has_prev)
        def _():
            copy_prev(s).wait_send()
            copy_next(s).wait_recv()
            high[slot, 0, :, bs:], low[slot, 0, :, bs:] = split(inbox[s, 0])

        @pl.when(has_next)
        def _():
            copy_next(s).wait_send()
            copy_prev(s).wait_recv()
            high[slot, rows + 1, :, : 2 * bs], low[slot, rows + 1, :, : 2 * bs] = split(inbox[s, 1])

        top, bottom = some_rows(slot, [0, rows - 1])

        @pl.when(s < ITERS - 1)
        def _():
            outbox[s + 1, 0] = top[:, : 2 * bs]
            outbox[s + 1, 1] = bottom[:, bs:]
            send(s + 1)

        lax.fori_loop(steps // 2, steps, inner, 0)
        return carry

    lax.fori_loop(0, ITERS, sweep, 0)

    def diagonal(i, carry):
        block = out_ref[i, W] + half
        out_ref[i, W] = block
        diag_ref[i] = jnp.sum(jnp.where(eye, block, 0.0), axis=0, keepdims=True)
        return carry

    lax.fori_loop(0, rows, diagonal, 0)


def purify(density, keep_mask, sizes):
    rows, band, bs = density.shape[:3]
    vmem, smem = pl.BlockSpec(memory_space=pltpu.VMEM), pl.BlockSpec(memory_space=pltpu.SMEM)
    return pl.pallas_call(
        functools.partial(purify_kernel, sizes),
        out_shape=(
            jax.ShapeDtypeStruct(density.shape, jnp.float32),
            jax.ShapeDtypeStruct((rows, 1, bs), jnp.float32),
        ),
        in_specs=[smem, vmem],
        out_specs=(vmem, vmem),
        scratch_shapes=[
            pltpu.VMEM((2, rows + 2, bs, band * bs), jnp.bfloat16),
            pltpu.VMEM((2, rows + 2, bs, band * bs), jnp.bfloat16),
            pltpu.VMEM((ITERS, 2, bs, (band - 1) * bs), jnp.float32),
            pltpu.VMEM((ITERS, 2, bs, (band - 1) * bs), jnp.float32),
            pltpu.SemaphoreType.DMA((ITERS, 2)),
            pltpu.SemaphoreType.DMA((ITERS, 2)),
        ],
        compiler_params=pltpu.CompilerParams(
            collective_id=0, has_side_effects=True, vmem_limit_bytes=40 * 1024 * 1024
        ),
        cost_estimate=pl.CostEstimate(
            flops=2 * 3 * 8 * 2 * ITERS * rows * bs**3, bytes_accessed=8 * density.size, transcendentals=0
        ),
    )(keep_mask, density)


def pair_kernel(cells, around_ref, own_ref, strength_ref, out_ref, spread):
    cells_x, cells_y, cells_z = cells
    atoms = own_ref.shape[2]
    step_y = cells_z + 2
    step_x = step_y * (cells_y + 2)
    ones = jnp.ones((8, atoms), jnp.float32)
    group = 32

    def one_cell(cell, carry):
        cx, cy, cz = cell // (cells_y * cells_z), (cell // cells_z) % cells_y, cell % cells_z
        corner = cx * step_x + cy * step_y + cz
        for axis in range(3):
            row = own_ref[axis, pl.ds(cell, 1), :]
            spread[axis] = jnp.transpose(jnp.broadcast_to(row, (atoms, atoms)))

        def one_group(g, c):
            here = pl.ds(pl.multiple_of(g * group, group), group)
            mine = [spread[axis, here, :] for axis in range(3)]
            sums = [jnp.zeros((group, atoms), jnp.float32) for _ in range(3)]
            for dx in range(3):
                for dy in range(3):
                    for dz in range(3):
                        at = pl.ds(corner + dx * step_x + dy * step_y + dz, 1)
                        gap = [mine[axis] - around_ref[axis, at, :] for axis in range(3)]
                        power = around_ref[3, at, :] - (gap[0] * gap[0] + gap[1] * gap[1] + gap[2] * gap[2])
                        weight = jnp.exp2(power)
                        sums = [sums[axis] + weight * gap[axis] for axis in range(3)]
            for axis in range(3):
                spread[3 + axis, here, :] = sums[axis]
            return c

        lax.fori_loop(0, atoms // group, one_group, 0)
        strength = strength_ref[pl.ds(cell, 1), :] * (1.0 / SCALE)
        for axis in range(3):
            summed = lax.dot_general(
                ones, spread[3 + axis], (((1,), (1,)), ((), ())),
                precision=lax.Precision.HIGHEST, preferred_element_type=jnp.float32)
            out_ref[axis, pl.ds(cell, 1), :] = summed[:1] * strength
        return carry

    lax.fori_loop(0, cells_x * cells_y * cells_z, one_cell, 0)


def embed_kernel(per_owner, list_ref, table_ref, coords_ref, charge_ref, pair_ref, out_ref):
    cells, atoms = charge_ref.shape
    slots = list_ref.shape[1]
    cell_ids = lax.broadcasted_iota(jnp.int32, (16, slots), 0)
    atom_ids = lax.broadcasted_iota(jnp.int32, (atoms, slots), 0)

    def one_owner(owner, sums):
        row = list_ref[pl.ds(owner, 1), :]
        in_cell = jnp.where(cell_ids == (row >> int(math.log2(atoms))), 1.0, 0.0).astype(jnp.bfloat16)
        in_slot = jnp.where(atom_ids == (row & (atoms - 1)), 1.0, 0.0).astype(jnp.bfloat16)
        times = lax.dot_general(in_cell, in_slot, (((1,), (1,)), ((), ())), preferred_element_type=jnp.float32)
        sums = list(sums)
        for part in range(per_owner // 8):
            start = pl.ds(pl.multiple_of(owner * per_owner + part * 8, 8), 8)
            table = table_ref[start, :]
            site = [jnp.broadcast_to(table[:, k : k + 1], (8, atoms)) for k in range(4)]
            for cell in range(cells):
                gap = [coords_ref[axis, cell : cell + 1, :] - site[axis] for axis in range(3)]
                square = gap[0] * gap[0] + gap[1] * gap[1] + gap[2] * gap[2] + SOFTEN
                root = lax.rsqrt(square)
                factor = (site[3] * times[cell : cell + 1, :]) * (root * root * root)
                for axis in range(3):
                    sums[axis * cells + cell] = sums[axis * cells + cell] + factor * gap[axis]
        return tuple(sums)

    zero = jnp.zeros((8, atoms), jnp.float32)
    sums = lax.fori_loop(0, list_ref.shape[0], one_owner, (zero,) * (3 * cells))
    for axis in range(3):
        for cell in range(cells):
            force = jnp.sum(sums[axis * cells + cell], axis=0, keepdims=True)
            out_ref[axis, cell : cell + 1, :] = (
                pair_ref[axis, cell : cell + 1, :] + EMBED * charge_ref[cell : cell + 1, :] * force
            )


def per_device(
    density, pattern, qm_sites, positions, atom_types, charges, eps_table, embed_atoms, embed_counts
):
    row_count = density.shape[0]
    axes = ("qrow", "qcol", "grp")
    sizes = tuple(lax.axis_size(axis) for axis in axes)
    device_count = sizes[0] * sizes[1] * sizes[2]
    first_row = lax.axis_index(axes) * row_count
    keep_mask = keep_of(pattern, first_row, row_count * device_count)
    grid_shape = positions.shape[1:]
    cells, atoms = grid_shape[:3], grid_shape[3]
    cell_count = cells[0] * cells[1] * cells[2]
    flat = (cell_count, atoms)

    type_ids = jnp.arange(eps_table.shape[0], dtype=jnp.int32)[:, None, None, None, None]
    strength = jnp.sqrt(
        jnp.sum(
            jnp.where(atom_types[None] == type_ids, eps_table[:, None, None, None, None], 0.0),
            axis=0,
        )
    )
    stacked = jnp.concatenate([positions, jnp.log2(strength)[None]], axis=0)
    extended = padded(stacked, (("qrow", 1), ("qcol", 2), ("grp", 3)), 1)
    wide = extended.shape[1:]
    around = jnp.concatenate(
        [
            jnp.stack(
                [
                    (extended[axis] + (lax.broadcasted_iota(jnp.int32, wide, axis) - 1).astype(jnp.float32)) * SCALE
                    for axis in range(3)
                ]
            ),
            extended[3:],
        ],
        axis=0,
    ).reshape(4, -1, atoms)
    local = [lax.broadcasted_iota(jnp.int32, grid_shape, axis) for axis in range(3)]
    own = jnp.stack([(positions[axis] + local[axis].astype(jnp.float32)) * SCALE for axis in range(3)])
    coords = jnp.stack(
        [
            positions[axis] + (local[axis] + lax.axis_index(axes[axis]) * cells[axis]).astype(jnp.float32)
            for axis in range(3)
        ]
    ).reshape((3,) + flat)

    current, diagonal = purify(density, keep_mask, sizes)
    qm_charge = qm_sites[3] - jnp.mean(diagonal[:, 0], axis=1)
    table = jnp.concatenate([qm_sites[:3], qm_charge[None]], axis=0).T
    table = lax.all_to_all(
        jnp.broadcast_to(table.reshape(1, -1), (device_count, table.size)), axes, 0, 0, tiled=True
    ).reshape(-1, 4)

    pair = pl.pallas_call(
        functools.partial(pair_kernel, cells),
        out_shape=jax.ShapeDtypeStruct((3,) + flat, jnp.float32),
        scratch_shapes=[pltpu.VMEM((6, atoms, atoms), jnp.float32)],
        compiler_params=pltpu.CompilerParams(vmem_limit_bytes=16 * 1024 * 1024),
        cost_estimate=pl.CostEstimate(
            flops=27 * 15 * cell_count * atoms * atoms, bytes_accessed=4 * around.size,
            transcendentals=27 * cell_count * atoms * atoms,
        ),
    )(around, own.reshape((3,) + flat), strength.reshape(flat))

    live = jnp.arange(embed_atoms.shape[2], dtype=jnp.int32)[None, :] < embed_counts[0][:, None]
    lists = jnp.where(live, embed_atoms[0], -1)
    force = pl.pallas_call(
        functools.partial(embed_kernel, row_count),
        out_shape=jax.ShapeDtypeStruct((3,) + flat, jnp.float32),
        compiler_params=pltpu.CompilerParams(vmem_limit_bytes=16 * 1024 * 1024),
    )(lists, table, coords, charges.reshape(flat), pair)
    return (current, force.reshape(positions.shape))


def solution(mesh):
    in_specs = (
        P(("qrow", "qcol", "grp"), None, None, None),
        P(("qrow", "qcol", "grp"), None),
        P(None, ("qrow", "qcol", "grp")),
        P(None, "qrow", "qcol", "grp", None),
        P("qrow", "qcol", "grp", None),
        P("qrow", "qcol", "grp", None),
        P(),
        P(("qrow", "qcol", "grp"), None, None),
        P(("qrow", "qcol", "grp"), None),
    )
    out_specs = (P(("qrow", "qcol", "grp"), None, None, None), P(None, "qrow", "qcol", "grp", None))
    return jax.shard_map(
        per_device, mesh=mesh, in_specs=in_specs, out_specs=out_specs, check_vma=False
    )
```

```python
import functools
import math

import jax
import jax.numpy as jnp
from jax import lax
from jax.experimental import pallas as pl
from jax.experimental.pallas import tpu as pltpu
from jax.sharding import PartitionSpec as P

W = 1
ITERS = 6


SIGMA_SQ = 0.25
EMBED = 20.0
SOFTEN = 1.0
MESH = pl.DeviceIdType.MESH
K_STACK = True
AT_ONCE = 2
SCALE = math.sqrt(1.0 / (SIGMA_SQ * math.log(2.0)))


def padded(cells, sides, width):
    for axis, dim in sides:
        count = lax.axis_size(axis)
        head = lax.slice_in_dim(cells, 0, width, axis=dim)
        tail = lax.slice_in_dim(cells, cells.shape[dim] - width, cells.shape[dim], axis=dim)
        cells = jnp.concatenate(
            [
                lax.ppermute(tail, axis, [(i, (i + 1) % count) for i in range(count)]),
                cells,
                lax.ppermute(head, axis, [((i + 1) % count, i) for i in range(count)]),
            ],
            axis=dim,
        )
    return cells


def keep_of(pattern, first_row, total_rows):
    row_ids = first_row + jnp.arange(pattern.shape[0], dtype=jnp.int32)[:, None]
    column_ids = row_ids + jnp.arange(pattern.shape[1], dtype=jnp.int32)[None, :] - W
    inside = (column_ids >= 0) & (column_ids < total_rows) & (pattern > 0)
    return jnp.where(inside, 1.0, 0.0).astype(jnp.float32)


def split(value):
    high = value.astype(jnp.bfloat16)
    return high, (value - high.astype(jnp.float32)).astype(jnp.bfloat16)


def purify_kernel(
    sizes, keep_ref, density_ref, out_ref, diag_ref, high, low, outbox, inbox, send_sem, recv_sem
):
    rows, bs = density_ref.shape[0], density_ref.shape[2]
    n_col, n_grp = sizes[1], sizes[2]
    total = sizes[0] * n_col * n_grp
    me = (lax.axis_index("qrow") * n_col + lax.axis_index("qcol")) * n_grp + lax.axis_index("grp")
    has_prev, has_next = me > 0, me < total - 1

    def place(index):
        return (index // (n_col * n_grp), (index // n_grp) % n_col, index % n_grp)

    to_prev, to_next = place(jnp.maximum(me - 1, 0)), place(jnp.minimum(me + 1, total - 1))

    def copy_prev(s):
        return pltpu.make_async_remote_copy(
            outbox.at[s, 0], inbox.at[s, 1], send_sem.at[s, 0], recv_sem.at[s, 1],
            device_id=to_prev, device_id_type=MESH)

    def copy_next(s):
        return pltpu.make_async_remote_copy(
            outbox.at[s, 1], inbox.at[s, 0], send_sem.at[s, 1], recv_sem.at[s, 0],
            device_id=to_next, device_id_type=MESH)

    barrier = pltpu.get_barrier_semaphore()

    @pl.when(has_prev)
    def _():
        pl.semaphore_signal(barrier, inc=1, device_id=to_prev, device_id_type=MESH)

    @pl.when(has_next)
    def _():
        pl.semaphore_signal(barrier, inc=1, device_id=to_next, device_id_type=MESH)

    eye = lax.broadcasted_iota(jnp.int32, (bs, bs), 0) == lax.broadcasted_iota(jnp.int32, (bs, bs), 1)
    half = jnp.where(eye, 0.5, 0.0)

    def masked(i):
        blocks = [density_ref[i, e] * keep_ref[i, e] for e in range(3)]
        blocks[W] = blocks[W] - half
        for e in range(3):
            out_ref[i, e] = blocks[e]
        return jnp.concatenate(blocks, axis=1)

    def put(slot, row, value):
        high[slot, row], low[slot, row] = split(value)

    first, last = masked(0), masked(rows - 1)
    outbox[0, 0] = first[:, : 2 * bs]
    outbox[0, 1] = last[:, bs:]
    put(0, 1, first)
    put(0, rows, last)

    pl.semaphore_wait(barrier, jnp.where(has_prev, 1, 0) + jnp.where(has_next, 1, 0))

    def send(s):
        @pl.when(has_prev)
        def _():
            copy_prev(s).start()

        @pl.when(has_next)
        def _():
            copy_next(s).start()

    send(0)
    edge = jnp.zeros((bs, 3 * bs), jnp.bfloat16)
    for slot in range(2):
        for row in (0, rows + 1):
            high[slot, row] = edge
            low[slot, row] = edge

    def fill(i, carry):
        put(0, i + 1, masked(i))
        return carry

    lax.fori_loop(1, rows - 1, fill, 0)

    def product(left, windows):
        left_high, left_low = left
        parts = []
        for tile in range(2):
            columns = slice(tile * bs, (tile + 2) * bs)
            wide_high, wide_low = windows[tile]
            if K_STACK:
                deep = jnp.concatenate([left_high[:, columns], left_low[:, columns], left_high[:, columns]], axis=1)
                wide = jnp.concatenate([wide_high, wide_high, wide_low], axis=0)
                parts.append(jnp.dot(deep, wide, preferred_element_type=jnp.float32))
            else:
                both = jnp.concatenate([left_high[:, columns], left_low[:, columns]], axis=0)
                by_high = jnp.dot(both, wide_high, preferred_element_type=jnp.float32)
                by_low = jnp.dot(left_high[:, columns], wide_low, preferred_element_type=jnp.float32)
                parts.append(by_high[:bs] + (by_high[bs:] + by_low))
        return [parts[0][:, :bs], parts[0][:, bs:] + parts[1][:, :bs], parts[1][:, bs:]]

    def window(store, slot, i):
        before, here, after = store.at[slot, i], store.at[slot, i + 1], store.at[slot, i + 2]
        one = jnp.concatenate([before[:, bs:], here[:, : 2 * bs]], axis=0)
        none = jnp.zeros((bs, bs), jnp.bfloat16)
        top = jnp.concatenate([none, here[:, 2 * bs :]], axis=1)
        return one, jnp.concatenate([top, after[:, : 2 * bs]], axis=0)

    def some_rows(slot, picked):
        windows = [list(zip(window(high, slot, i), window(low, slot, i))) for i in picked]
        keeps = [[keep_ref[i, e] for e in range(3)] for i in picked]
        squares = []
        for i, pieces, keep in zip(picked, windows, keeps):
            blocks = product((high[slot, i + 1], low[slot, i + 1]), pieces)
            squares.append(split(jnp.concatenate([keep[e] * blocks[e] for e in range(3)], axis=1)))
        cubes = [product(square, pieces) for square, pieces in zip(squares, windows)]
        results = []
        for i, cube, keep in zip(picked, cubes, keeps):
            fresh = [1.5 * out_ref[i, e] - (2.0 * keep[e]) * cube[e] for e in range(3)]
            results.append((fresh, split(jnp.concatenate(fresh, axis=1))))
        for i, (fresh, (fresh_high, fresh_low)) in zip(picked, results):
            for e in range(3):
                out_ref[i, e] = fresh[e]
            high[1 - slot, i + 1] = fresh_high
            low[1 - slot, i + 1] = fresh_low
        return [jnp.concatenate(fresh, axis=1) for fresh, _ in results]

    steps = (rows - 2) // AT_ONCE

    def sweep(s, carry):
        slot = lax.rem(s, 2)

        def inner(i, c):
            some_rows(slot, [1 + AT_ONCE * i + k for k in range(AT_ONCE)])
            return c

        lax.fori_loop(0, steps // 2, inner, 0)

        @pl.when(has_prev)
        def _():
            copy_prev(s).wait_send()
            copy_next(s).wait_recv()
            high[slot, 0, :, bs:], low[slot, 0, :, bs:] = split(inbox[s, 0])

        @pl.when(has_next)
        def _():
            copy_next(s).wait_send()
            copy_prev(s).wait_recv()
            high[slot, rows + 1, :, : 2 * bs], low[slot, rows + 1, :, : 2 * bs] = split(inbox[s, 1])

        top, bottom = some_rows(slot, [0, rows - 1])

        @pl.when(s < ITERS - 1)
        def _():
            outbox[s + 1, 0] = top[:, : 2 * bs]
            outbox[s + 1, 1] = bottom[:, bs:]
            send(s + 1)

        lax.fori_loop(steps // 2, steps, inner, 0)
        return carry

    lax.fori_loop(0, ITERS, sweep, 0)

    def diagonal(i, carry):
        block = out_ref[i, W] + half
        out_ref[i, W] = block
        diag_ref[i] = jnp.sum(jnp.where(eye, block, 0.0), axis=0, keepdims=True)
        return carry

    lax.fori_loop(0, rows, diagonal, 0)


def purify(density, keep_mask, sizes):
    rows, band, bs = density.shape[:3]
    vmem, smem = pl.BlockSpec(memory_space=pltpu.VMEM), pl.BlockSpec(memory_space=pltpu.SMEM)
    return pl.pallas_call(
        functools.partial(purify_kernel, sizes),
        out_shape=(
            jax.ShapeDtypeStruct(density.shape, jnp.float32),
            jax.ShapeDtypeStruct((rows, 1, bs), jnp.float32),
        ),
        in_specs=[smem, vmem],
        out_specs=(vmem, vmem),
        scratch_shapes=[
            pltpu.VMEM((2, rows + 2, bs, band * bs), jnp.bfloat16),
            pltpu.VMEM((2, rows + 2, bs, band * bs), jnp.bfloat16),
            pltpu.VMEM((ITERS, 2, bs, (band - 1) * bs), jnp.float32),
            pltpu.VMEM((ITERS, 2, bs, (band - 1) * bs), jnp.float32),
            pltpu.SemaphoreType.DMA((ITERS, 2)),
            pltpu.SemaphoreType.DMA((ITERS, 2)),
        ],
        compiler_params=pltpu.CompilerParams(
            collective_id=0, has_side_effects=True, vmem_limit_bytes=40 * 1024 * 1024
        ),
        cost_estimate=pl.CostEstimate(
            flops=2 * 3 * 8 * 2 * ITERS * rows * bs**3, bytes_accessed=8 * density.size, transcendentals=0
        ),
    )(keep_mask, density)


def pair_kernel(cells, around_ref, own_ref, strength_ref, out_ref, spread):
    cells_x, cells_y, cells_z = cells
    atoms = own_ref.shape[2]
    step_y = cells_z + 2
    step_x = step_y * (cells_y + 2)
    ones = jnp.ones((8, atoms), jnp.float32)
    group = 32

    def one_cell(cell, carry):
        cx, cy, cz = cell // (cells_y * cells_z), (cell // cells_z) % cells_y, cell % cells_z
        corner = cx * step_x + cy * step_y + cz
        for axis in range(3):
            row = own_ref[axis, pl.ds(cell, 1), :]
            spread[axis] = jnp.transpose(jnp.broadcast_to(row, (atoms, atoms)))

        def one_group(g, c):
            here = pl.ds(pl.multiple_of(g * group, group), group)
            mine = [spread[axis, here, :] for axis in range(3)]
            sums = [jnp.zeros((group, atoms), jnp.float32) for _ in range(3)]
            for dx in range(3):
                for dy in range(3):
                    for dz in range(3):
                        at = pl.ds(corner + dx * step_x + dy * step_y + dz, 1)
                        gap = [mine[axis] - around_ref[axis, at, :] for axis in range(3)]
                        power = around_ref[3, at, :] - (gap[0] * gap[0] + gap[1] * gap[1] + gap[2] * gap[2])
                        weight = jnp.exp2(power)
                        sums = [sums[axis] + weight * gap[axis] for axis in range(3)]
            for axis in range(3):
                spread[3 + axis, here, :] = sums[axis]
            return c

        lax.fori_loop(0, atoms // group, one_group, 0)
        strength = strength_ref[pl.ds(cell, 1), :] * (1.0 / SCALE)
        for axis in range(3):
            summed = lax.dot_general(
                ones, spread[3 + axis], (((1,), (1,)), ((), ())),
                precision=lax.Precision.HIGHEST, preferred_element_type=jnp.float32)
            out_ref[axis, pl.ds(cell, 1), :] = summed[:1] * strength
        return carry

    lax.fori_loop(0, cells_x * cells_y * cells_z, one_cell, 0)


def embed_kernel(per_owner, list_ref, table_ref, coords_ref, charge_ref, pair_ref, out_ref):
    cells, atoms = charge_ref.shape
    slots = list_ref.shape[1]
    cell_ids = lax.broadcasted_iota(jnp.int32, (16, slots), 0)
    atom_ids = lax.broadcasted_iota(jnp.int32, (atoms, slots), 0)

    def one_owner(owner, sums):
        row = list_ref[pl.ds(owner, 1), :]
        in_cell = jnp.where(cell_ids == (row >> int(math.log2(atoms))), 1.0, 0.0).astype(jnp.bfloat16)
        in_slot = jnp.where(atom_ids == (row & (atoms - 1)), 1.0, 0.0).astype(jnp.bfloat16)
        times = lax.dot_general(in_cell, in_slot, (((1,), (1,)), ((), ())), preferred_element_type=jnp.float32)
        sums = list(sums)
        for part in range(per_owner // 8):
            start = pl.ds(pl.multiple_of(owner * per_owner + part * 8, 8), 8)
            table = table_ref[start, :]
            site = [jnp.broadcast_to(table[:, k : k + 1], (8, atoms)) for k in range(4)]
            for cell in range(cells):
                gap = [coords_ref[axis, cell : cell + 1, :] - site[axis] for axis in range(3)]
                square = gap[0] * gap[0] + gap[1] * gap[1] + gap[2] * gap[2] + SOFTEN
                root = lax.rsqrt(square)
                factor = (site[3] * times[cell : cell + 1, :]) * (root * root * root)
                for axis in range(3):
                    sums[axis * cells + cell] = sums[axis * cells + cell] + factor * gap[axis]
        return tuple(sums)

    zero = jnp.zeros((8, atoms), jnp.float32)
    sums = lax.fori_loop(0, list_ref.shape[0], one_owner, (zero,) * (3 * cells))
    for axis in range(3):
        for cell in range(cells):
            force = jnp.sum(sums[axis * cells + cell], axis=0, keepdims=True)
            out_ref[axis, cell : cell + 1, :] = (
                pair_ref[axis, cell : cell + 1, :] + EMBED * charge_ref[cell : cell + 1, :] * force
            )


def per_device(
    density, pattern, qm_sites, positions, atom_types, charges, eps_table, embed_atoms, embed_counts
):
    row_count = density.shape[0]
    axes = ("qrow", "qcol", "grp")
    sizes = tuple(lax.axis_size(axis) for axis in axes)
    device_count = sizes[0] * sizes[1] * sizes[2]
    first_row = lax.axis_index(axes) * row_count
    keep_mask = keep_of(pattern, first_row, row_count * device_count)
    grid_shape = positions.shape[1:]
    cells, atoms = grid_shape[:3], grid_shape[3]
    cell_count = cells[0] * cells[1] * cells[2]
    flat = (cell_count, atoms)

    type_ids = jnp.arange(eps_table.shape[0], dtype=jnp.int32)[:, None, None, None, None]
    strength = jnp.sqrt(
        jnp.sum(
            jnp.where(atom_types[None] == type_ids, eps_table[:, None, None, None, None], 0.0),
            axis=0,
        )
    )
    stacked = jnp.concatenate([positions, jnp.log2(strength)[None]], axis=0)
    extended = padded(stacked, (("qrow", 1), ("qcol", 2), ("grp", 3)), 1)
    wide = extended.shape[1:]
    around = jnp.concatenate(
        [
            jnp.stack(
                [
                    (extended[axis] + (lax.broadcasted_iota(jnp.int32, wide, axis) - 1).astype(jnp.float32)) * SCALE
                    for axis in range(3)
                ]
            ),
            extended[3:],
        ],
        axis=0,
    ).reshape(4, -1, atoms)
    local = [lax.broadcasted_iota(jnp.int32, grid_shape, axis) for axis in range(3)]
    own = jnp.stack([(positions[axis] + local[axis].astype(jnp.float32)) * SCALE for axis in range(3)])
    coords = jnp.stack(
        [
            positions[axis] + (local[axis] + lax.axis_index(axes[axis]) * cells[axis]).astype(jnp.float32)
            for axis in range(3)
        ]
    ).reshape((3,) + flat)

    keep_mask, around = lax.optimization_barrier((keep_mask, around))
    current, diagonal = purify(density, keep_mask, sizes)
    qm_charge = qm_sites[3] - jnp.mean(diagonal[:, 0], axis=1)
    table = jnp.concatenate([qm_sites[:3], qm_charge[None]], axis=0).T
    table = lax.all_to_all(
        jnp.broadcast_to(table.reshape(1, -1), (device_count, table.size)), axes, 0, 0, tiled=True
    ).reshape(-1, 4)

    pair = pl.pallas_call(
        functools.partial(pair_kernel, cells),
        out_shape=jax.ShapeDtypeStruct((3,) + flat, jnp.float32),
        scratch_shapes=[pltpu.VMEM((6, atoms, atoms), jnp.float32)],
        compiler_params=pltpu.CompilerParams(vmem_limit_bytes=16 * 1024 * 1024),
        cost_estimate=pl.CostEstimate(
            flops=27 * 15 * cell_count * atoms * atoms, bytes_accessed=4 * around.size,
            transcendentals=27 * cell_count * atoms * atoms,
        ),
    )(around, own.reshape((3,) + flat), strength.reshape(flat))

    live = jnp.arange(embed_atoms.shape[2], dtype=jnp.int32)[None, :] < embed_counts[0][:, None]
    lists = jnp.where(live, embed_atoms[0], -1)
    force = pl.pallas_call(
        functools.partial(embed_kernel, row_count),
        out_shape=jax.ShapeDtypeStruct((3,) + flat, jnp.float32),
        compiler_params=pltpu.CompilerParams(vmem_limit_bytes=16 * 1024 * 1024),
    )(lists, table, coords, charges.reshape(flat), pair)
    return (current, force.reshape(positions.shape))


def solution(mesh):
    in_specs = (
        P(("qrow", "qcol", "grp"), None, None, None),
        P(("qrow", "qcol", "grp"), None),
        P(None, ("qrow", "qcol", "grp")),
        P(None, "qrow", "qcol", "grp", None),
        P("qrow", "qcol", "grp", None),
        P("qrow", "qcol", "grp", None),
        P(),
        P(("qrow", "qcol", "grp"), None, None),
        P(("qrow", "qcol", "grp"), None),
    )
    out_specs = (P(("qrow", "qcol", "grp"), None, None, None), P(None, "qrow", "qcol", "grp", None))
    return jax.shard_map(
        per_device, mesh=mesh, in_specs=in_specs, out_specs=out_specs, check_vma=False
    )
```
